32 devices in a mesh: gx: 8 (over z, x), gy: 4 (over y, core).
Axes of the slice: x: 2, y: 2, z: 4, core: 2. Of those that a mesh axis runs over, the one named last changes fastest.
Arguments:
- tracers: float32 [2, 80, 128, 512], P(None, None, 'gx', 'gy'), may hold values from -6 to 6
- velocity: float32 [2, 80, 128, 512], P(None, None, 'gx', 'gy'), may hold values from -0.4 to 0.4
- mixing: float32 [79, 128, 512], P(None, 'gx', 'gy'), may hold values from 0.05 to 5
- levels: int32 [128, 512], P('gx', 'gy'), may hold values from 0 to 80, as said below
- surface: float32 [128, 512], P('gx', 'gy'), may hold values from -6 to 6
- transport: float32 [2, 128, 512], P(None, 'gx', 'gy'), may hold values from -1.5 to 1.5
- forcing: float32 [2, 128, 512], P(None, 'gx', 'gy'), may hold values from -1 to 1
Outputs:
- surface_next: float32 [128, 512], P('gx', 'gy')
- transport_next: float32 [2, 128, 512], P(None, 'gx', 'gy')
- mean_transport: float32 [2, 128, 512], P(None, 'gx', 'gy')
- tracers_next: float32 [2, 80, 128, 512], P(None, None, 'gx', 'gy')
The draws below stay inside these ranges and needn't reach their ends.
Inputs may be any that keep to these rules, and one draw needn't show every extreme that they name: levels is 0 on land columns and 80 on columns that reach the full depth; other columns are shallower.
All inputs are finite; a program needn't handle non-finite values.
Results may differ from the reference program's by a relative error of at most 0.0003.
Values sent between devices are 32-bit elements; how exact they have to be, the bound alone decides.
A program may use at most 128 MiB of HBM per device.

```python
import math
import jax
import jax.numpy as jnp
from jax import lax

CX = 16
K = 80
BT_STEPS = 24
NX = 128
NY = 512


def draw_levels(key, part):
    roll = jax.random.randint(jax.random.fold_in(key, 11), (NX, NY), 0, 1000)
    shallow = jax.random.randint(jax.random.fold_in(key, 12), (NX, NY), 1, K)
    full = jnp.full((NX, NY), K, dtype=jnp.int32)
    land = jnp.zeros((NX, NY), dtype=jnp.int32)
    return jnp.where(roll < 30, land, jnp.where(roll < 80, shallow, full)).astype(jnp.int32)


def block_levels(own_key, shape, shards, smallest, top_value):
    loudness = 1.0
    for dim, shards_of in shards:
        steps = jax.random.uniform(jax.random.fold_in(jax.random.fold_in(own_key, 6), dim), (shards_of,), jnp.float32, smallest / len(shards), top_value / len(shards))
        loudness = loudness * jnp.repeat(jnp.exp(steps), shape[dim] // shards_of).reshape((-1,) + (1,) * (len(shape) - 1 - dim))
    return loudness


def bell_draw(key, extent, scale, most, split=(), held_as=jnp.bfloat16):
    array = scale * jax.random.normal(key, extent, jnp.float32)
    if split:
        array = array * block_levels(key, extent, split, -0.22, 0.18)
    return jnp.clip(array, -most, most).astype(held_as)


def setup_inputs(seed: int = 0) -> dict:
    key_of = jax.random.split(jax.random.key(seed), 8)
    return {
        "tracers": bell_draw(key_of[0], (2, K, NX, NY), 1.0, 6.0, ((2, 8), (3, 4)), jnp.float32),
        "velocity": bell_draw(key_of[1], (2, K, NX, NY), 0.1, 0.4, ((2, 8), (3, 4)), jnp.float32),
        "mixing": jnp.clip(jnp.exp(math.log(5.0) - 4.6051702 * jax.random.uniform(key_of[2], (K - 1, NX, NY), jnp.float32) ** block_levels(key_of[2], (K - 1, NX, NY), ((1, 8), (2, 4)), -0.2, 0.2)), 0.05, 5.0),
        "levels": draw_levels(jax.random.fold_in(key_of[7], 71), 0),
        "surface": bell_draw(key_of[4], (NX, NY), 1.0, 6.0, ((0, 8), (1, 4)), jnp.float32),
        "transport": bell_draw(key_of[5], (2, NX, NY), 0.3, 1.5, ((1, 8), (2, 4)), jnp.float32),
        "forcing": bell_draw(key_of[6], (2, NX, NY), 0.2, 1.0, ((1, 8), (2, 4)), jnp.float32),
    }


height_rate = 0.5
gravity_rate = 0.9
advect_scale = 0.01


def from_lower(field, axis):
    widths = [(0, 0)] * field.ndim
    widths[axis] = (1, 0)
    padded = jnp.pad(field, widths)
    return lax.slice_in_dim(padded, 0, field.shape[axis], axis=axis)


def from_upper(field, axis):
    widths = [(0, 0)] * field.ndim
    widths[axis] = (0, 1)
    padded = jnp.pad(field, widths)
    return lax.slice_in_dim(padded, 1, field.shape[axis] + 1, axis=axis)


def upwind_change(padded, speed, axis, count):
    parts = [lax.slice_in_dim(padded, offset, offset + count + 1, axis=axis) for offset in range(6)]
    plus = (2.0 * parts[0] - 13.0 * parts[1] + 47.0 * parts[2] + 27.0 * parts[3] - 3.0 * parts[4]) / 60.0
    minus = (2.0 * parts[5] - 13.0 * parts[4] + 47.0 * parts[3] + 27.0 * parts[2] - 3.0 * parts[1]) / 60.0
    flux = speed * jnp.where(speed > 0.0, plus, minus)
    return lax.slice_in_dim(flux, 1, count + 1, axis=axis) - lax.slice_in_dim(flux, 0, count, axis=axis)


def column_solve(source, coupling):
    depth_count = source.shape[1]
    gains = []
    values = []
    for level in range(depth_count):
        if level < depth_count - 1:
            upper = coupling[level]
        else:
            upper = jnp.zeros_like(coupling[0])
        if level == 0:
            pivot = 1.0 + upper
            value = source[:, 0] / pivot
        else:
            lower = coupling[level - 1]
            pivot = 1.0 + lower + upper - lower * gains[-1]
            value = (source[:, level] + lower * values[-1]) / pivot
        gains.append(upper / pivot)
        values.append(value)
    result = [None] * depth_count
    result[depth_count - 1] = values[depth_count - 1]
    for level in range(depth_count - 2, -1, -1):
        result[level] = values[level] + gains[level] * result[level + 1]
    return jnp.stack(result, axis=1)


def reference(tracers, velocity, mixing, levels, surface, transport, forcing):
    depth = levels.astype(jnp.float32) / K
    east_depth = jnp.minimum(depth, from_upper(depth, 0))
    north_depth = jnp.minimum(depth, from_upper(depth, 1))
    east_wet = (east_depth > 0.0).astype(jnp.float32)
    north_wet = (north_depth > 0.0).astype(jnp.float32)
    height = surface
    east_flow = transport[0] * east_wet
    north_flow = transport[1] * north_wet
    east_total = jnp.zeros_like(height)
    north_total = jnp.zeros_like(height)
    for substep in range(BT_STEPS):
        height = height - height_rate * ((east_flow - from_lower(east_flow, 0)) + (north_flow - from_lower(north_flow, 1)))
        east_flow = east_wet * (east_flow - gravity_rate * east_depth * (from_upper(height, 0) - height) + height_rate * east_depth * forcing[0])
        north_flow = north_wet * (north_flow - gravity_rate * north_depth * (from_upper(height, 1) - height) + height_rate * north_depth * forcing[1])
        east_total = east_total + east_flow
        north_total = north_total + north_flow
    east_mean = east_total / BT_STEPS
    north_mean = north_total / BT_STEPS
    east_speed = advect_scale * east_mean / jnp.maximum(east_depth, 1.0 / K)
    north_speed = advect_scale * north_mean / jnp.maximum(north_depth, 1.0 / K)

    def level_step(level):
        layer = lax.dynamic_index_in_dim(tracers, level, 1, keepdims=False)
        shear = lax.dynamic_index_in_dim(velocity, level, 1, keepdims=False)
        middle = (level.astype(jnp.float32) + 0.5) / K
        east_face = (shear[0] + east_speed) * (middle < east_depth).astype(jnp.float32)
        north_face = (shear[1] + north_speed) * (middle < north_depth).astype(jnp.float32)
        east_face = jnp.concatenate([jnp.zeros_like(east_face[:1]), east_face], axis=0)
        north_face = jnp.concatenate([jnp.zeros_like(north_face[:, :1]), north_face], axis=1)
        padded_x = jnp.pad(layer, ((0, 0), (3, 3), (0, 0)))
        padded_y = jnp.pad(layer, ((0, 0), (0, 0), (3, 3)))
        change = upwind_change(padded_x, east_face[None], 1, NX) + upwind_change(padded_y, north_face[None], 2, NY)
        return layer - change

    stepped = lax.map(level_step, jnp.arange(K, dtype=jnp.int32))

    def block_mix(block):
        start = block * CX
        rows = lax.dynamic_slice_in_dim(stepped, start, CX, 2)
        source = jnp.moveaxis(rows, 0, 1)
        rates = lax.dynamic_slice_in_dim(mixing, start, CX, 1)
        depths = lax.dynamic_slice_in_dim(levels, start, CX, 0)
        above = jnp.arange(1, K, dtype=jnp.int32)[:, None, None] < depths[None]
        return column_solve(source, rates * above.astype(jnp.float32))

    blocks = lax.map(block_mix, jnp.arange(NX // CX, dtype=jnp.int32))
    mixed = jnp.moveaxis(blocks, 0, 2).reshape(2, K, NX, NY)
    return height, jnp.stack([east_flow, north_flow]), jnp.stack([east_mean, north_mean]), mixed
```

```python
import functools

import jax
import jax.numpy as jnp
from jax import lax
from jax.experimental import pallas as pl
from jax.experimental.pallas import tpu as pltpu
from jax.sharding import PartitionSpec as P

K = 80
STEPS = 24
CX = 16
CY = 128
GROUP = 8
GROUPS = K // GROUP
CHUNKS = 5
CHUNK = GROUPS // CHUNKS
ROWS = 72
OWN = 32
EAST_ROWS = 7 * GROUP
WEST_ROWS = 6 * GROUP
MESH = pl.DeviceIdType.MESH

DIRECTIONS = [(dx, dy) for dx in (1, -1, 2, -2, 0) for dy in (0, 1, -1) if (dx, dy) != (0, 0)]


def roll(x, shift, axis):
    return pltpu.roll(x, shift % x.shape[axis], axis)


def kernel(
    nx, ny,
    tracers, velocity, mixing, levels, surface, transport, forcing,
    surface_out, transport_out, mean_out, tracers_out,
    fields, pack_w, pack_e, halo_e, halo_w, lev,
    text, velx, vely, mix, gain, lower, inverse, values,
    east_send, west_send, east_recv, west_recv,
    north_send, south_send, north_recv, south_recv,
    coef, state,
    local_sem, out_sem, b_send, b_recv, x_send, x_recv, y_send, y_recv,
):
    gx = lax.axis_index("gx")
    gy = lax.axis_index("gy")

    def has(dx, dy):
        x, y = gx + dx, gy + dy
        return (x >= 0) & (x < nx) & (y >= 0) & (y < ny)

    def device(dx, dy):
        return (lax.rem(gx + dx + nx, nx), lax.rem(gy + dy + ny, ny))

    own = pl.ds(OWN, CX)
    loads = [
        pltpu.make_async_copy(surface, fields.at[0, own, :], local_sem.at[0]),
        pltpu.make_async_copy(transport, fields.at[1:3, own, :], local_sem.at[1]),
        pltpu.make_async_copy(forcing, fields.at[3:5, own, :], local_sem.at[2]),
        pltpu.make_async_copy(levels, lev, local_sem.at[3]),
        pltpu.make_async_copy(tracers, text.at[:, :, 8:24, :], local_sem.at[4]),
        pltpu.make_async_copy(velocity.at[0], velx.at[:, 8:24, :], local_sem.at[5]),
        pltpu.make_async_copy(velocity.at[1], vely, local_sem.at[6]),
        pltpu.make_async_copy(mixing, mix.at[0 : K - 1], local_sem.at[7]),
    ]
    for load in loads:
        load.start()

    barrier = pltpu.get_barrier_semaphore()
    count = jnp.int32(0)
    for dx, dy in DIRECTIONS:
        there = has(dx, dy)

        @pl.when(there)
        def _():
            pl.semaphore_signal(barrier, inc=1, device_id=device(dx, dy), device_id_type=MESH)

        count = count + there.astype(jnp.int32)

    lane = lax.broadcasted_iota(jnp.int32, (CX, CY), 1)

    for load in loads[:4]:
        load.wait()
    fields[5, OWN : OWN + CX, :] = lev[...].astype(jnp.float32) * (1.0 / K)
    for group in range(2):
        east = None
        west = None
        for slot in range(4 if group == 0 else 2):
            x = fields[4 * group + slot, OWN : OWN + CX, :]
            inside = (lane >= 32 * slot) & (lane < 32 * slot + 32)
            to_east = roll(x, 32 * slot + 32, 1)
            to_west = roll(x, 32 * slot, 1)
            east = to_east if east is None else jnp.where(inside, to_east, east)
            west = to_west if west is None else jnp.where(inside, to_west, west)
        pack_e[group] = east
        pack_w[group] = west

    def barotropic_copy(index):
        dx, dy = DIRECTIONS[index]
        rows = 8 if dx == -2 else CX
        start = CX * (2 - dx)
        if dy == 0:
            src, dst = fields.at[:, pl.ds(OWN, rows), :], fields
        elif dy == 1:
            src, dst = pack_e.at[:, pl.ds(0, rows), :], halo_w
        else:
            src, dst = pack_w.at[:, pl.ds(0, rows), :], halo_e
        return (
            pltpu.make_async_remote_copy(
                src_ref=src,
                dst_ref=dst.at[:, pl.ds(start, rows), :],
                send_sem=b_send.at[index],
                recv_sem=b_recv.at[index],
                device_id=device(dx, dy),
                device_id_type=MESH,
            ),
            dst,
            start,
            rows,
        )

    def x_copy(direction, chunk):
        src, dst, dx = ((east_send, east_recv, 1), (west_send, west_recv, -1))[direction]
        part = pl.ds(chunk * CHUNK, CHUNK)
        return pltpu.make_async_remote_copy(
            src_ref=src.at[part], dst_ref=dst.at[part],
            send_sem=x_send.at[direction, chunk], recv_sem=x_recv.at[direction, chunk],
            device_id=device(dx, 0), device_id_type=MESH,
        ), dst, part, dx

    def y_copy(direction):
        src, dst, dy = ((north_send, north_recv, 1), (south_send, south_recv, -1))[direction]
        return pltpu.make_async_remote_copy(
            src_ref=src, dst_ref=dst,
            send_sem=y_send.at[direction], recv_sem=y_recv.at[direction],
            device_id=device(0, dy), device_id_type=MESH,
        ), dst, dy

    pl.semaphore_wait(barrier, count)
    for index, (dx, dy) in enumerate(DIRECTIONS):
        copy, dst, start, rows = barotropic_copy(index)
        pl.when(has(dx, dy))(copy.start)

        @pl.when(jnp.logical_not(has(-dx, -dy)))
        def _():
            dst[:, pl.ds(start, rows), :] = jnp.zeros((dst.shape[0], rows, CY), jnp.float32)

    for load in loads[4:7]:
        load.wait()

    def pack_x(g, carry):
        for l in range(GROUP):
            k = g * GROUP + l
            for t in range(2):
                east_send[g, 7 * l + 3 * t : 7 * l + 3 * t + 3, :] = text[t, k, 21:24, :]
                west_send[g, 6 * l + 3 * t : 6 * l + 3 * t + 3, :] = text[t, k, 8:11, :]
            east_send[g, 7 * l + 6 : 7 * l + 7, :] = velx[k, 23:24, :]
        return carry

    for chunk in range(CHUNKS):
        lax.fori_loop(chunk * CHUNK, chunk * CHUNK + CHUNK, pack_x, 0)
        for direction in range(2):
            copy, dst, part, dx = x_copy(direction, chunk)
            pl.when(has(dx, 0))(copy.start)

            @pl.when(jnp.logical_not(has(-dx, 0)))
            def _():
                dst[part] = jnp.zeros((CHUNK,) + dst.shape[1:], jnp.float32)

    def pack_y(g, carry):
        north = jnp.zeros((CX, CY), jnp.float32)
        south = jnp.zeros((CX, CY), jnp.float32)
        for l in range(GROUP):
            k = g * GROUP + l
            t0 = text[0, k, 8:24, :]
            t1 = text[1, k, 8:24, :]
            high = jnp.where(
                lane >= 125, t0,
                jnp.where(lane >= 122, roll(t1, -3, 1), jnp.where(lane == 121, roll(vely[k], -6, 1), 0.0)),
            )
            low = jnp.where(lane < 3, t0, jnp.where(lane < 6, roll(t1, 3, 1), 0.0))
            north = north + roll(high, 16 * l + 8, 1)
            south = south + roll(low, 16 * l, 1)
        north_send[g] = north
        south_send[g] = south
        return carry

    lax.fori_loop(0, GROUPS, pack_y, 0)
    for direction in range(2):
        copy, dst, dy = y_copy(direction)
        pl.when(has(0, dy))(copy.start)

        @pl.when(jnp.logical_not(has(0, -dy)))
        def _():
            dst[...] = jnp.zeros(dst.shape, jnp.float32)

    loads[7].wait()
    mix[K - 1] = jnp.zeros((CX, CY), jnp.float32)

    def factor(k, carry):
        below, previous = carry
        upper = jnp.where(k + 1 < lev[...], mix[k], 0.0)
        inv = 1.0 / (1.0 + below + upper - below * previous)
        g = upper * inv
        gain[k] = g
        inverse[k] = inv
        lower[k] = below * inv
        return upper, g

    zero = jnp.zeros((CX, CY), jnp.float32)
    lax.fori_loop(0, K, factor, (zero, zero), unroll=4)

    for index, (dx, dy) in enumerate(DIRECTIONS):
        copy = barotropic_copy(index)[0]
        pl.when(has(-dx, -dy))(copy.wait_recv)

    wide = lax.broadcasted_iota(jnp.int32, (ROWS, CY), 1)

    def beside(index):
        group, slot = divmod(index, 4)
        return jnp.where(
            wide < 64, roll(halo_e[group], -32 * slot, 1), roll(halo_w[group], 96 - 32 * slot, 1)
        )

    def upper_x(pair):
        return tuple(roll(x, -1, 0) for x in pair)

    def lower_x(pair):
        return tuple(roll(x, 1, 0) for x in pair)

    def upper_y(pair):
        a, b = (roll(x, -1, 1) for x in pair)
        return jnp.where(wide == CY - 1, b, a), jnp.where(wide == CY - 1, a, b)

    def lower_y(pair):
        a, b = (roll(x, 1, 1) for x in pair)
        return jnp.where(wide == 0, b, a), jnp.where(wide == 0, a, b)

    depth = (fields[5], beside(5))
    east_depth = tuple(jnp.minimum(a, b) for a, b in zip(depth, upper_x(depth)))
    north_depth = tuple(jnp.minimum(a, b) for a, b in zip(depth, upper_y(depth)))
    for tile in range(2):
        other = (lambda i: fields[i]) if tile == 0 else beside
        coef[0, tile] = 0.9 * east_depth[tile]
        coef[1, tile] = 0.5 * east_depth[tile] * other(3)
        coef[2, tile] = 0.9 * north_depth[tile]
        coef[3, tile] = 0.5 * north_depth[tile] * other(4)
        coef[4, tile] = east_depth[tile]
        coef[5, tile] = north_depth[tile]
        state[0, tile] = other(0)
        state[1, tile] = jnp.where(east_depth[tile] > 0.0, other(1), 0.0)
        state[2, tile] = jnp.where(north_depth[tile] > 0.0, other(2), 0.0)
        state[3, tile] = jnp.zeros((ROWS, CY), jnp.float32)
        state[4, tile] = jnp.zeros((ROWS, CY), jnp.float32)

    def substep(step, carry):
        east = (state[1, 0], state[1, 1])
        north = (state[2, 0], state[2, 1])
        east_low = lower_x(east)
        north_low = lower_y(north)
        height = tuple(
            state[0, i] - 0.5 * ((east[i] - east_low[i]) + (north[i] - north_low[i])) for i in range(2)
        )
        high_x = upper_x(height)
        high_y = upper_y(height)
        for i in range(2):
            state[0, i] = height[i]
            e = east[i] - coef[0, i] * (high_x[i] - height[i]) + coef[1, i]
            n = north[i] - coef[2, i] * (high_y[i] - height[i]) + coef[3, i]
            state[1, i] = e
            state[2, i] = n
            state[3, i] = state[3, i] + e
            state[4, i] = state[4, i] + n
        return carry

    lax.fori_loop(0, STEPS, substep, 0)

    surface_out[...] = state[0, 0, OWN : OWN + CX, :]
    transport_out[0] = state[1, 0, OWN : OWN + CX, :]
    transport_out[1] = state[2, 0, OWN : OWN + CX, :]
    mean_out[0] = state[3, 0, OWN : OWN + CX, :] * (1.0 / STEPS)
    mean_out[1] = state[4, 0, OWN : OWN + CX, :] * (1.0 / STEPS)

    scale = 0.01 / STEPS
    for i in range(2):
        state[3, i] = scale * state[3, i] / jnp.maximum(coef[4, i], 1.0 / K)
        state[4, i] = scale * state[4, i] / jnp.maximum(coef[5, i], 1.0 / K)

    here = slice(OWN, OWN + CX)
    behind = slice(OWN - 1, OWN + CX - 1)
    east_speed, west_speed = state[3, 0, here, :], state[3, 0, behind, :]
    east_limit, west_limit = coef[4, 0, here, :], coef[4, 0, behind, :]
    north_speed, north_limit = state[4, 0, here, :], coef[5, 0, here, :]
    south_speed = jnp.where(lane == 0, roll(state[4, 1, here, :], 1, 1), roll(north_speed, 1, 1))
    south_limit = jnp.where(lane == 0, roll(coef[5, 1, here, :], 1, 1), roll(north_limit, 1, 1))

    for direction in range(2):
        copy, dst, dy = y_copy(direction)
        pl.when(has(0, -dy))(copy.wait_recv)

    def flux(cells, w, size):
        a, b, c, d, e, f = cells
        even = (a + f) - 8.0 * (b + e) + 37.0 * (c + d)
        odd = (a - f) - 5.0 * (b - e) + 10.0 * (c - d)
        return w * even + size * odd

    def face(mid, limit, value):
        w = jnp.where(mid < limit, value, 0.0) * (1.0 / 60.0)
        return w, jnp.abs(w)

    def advance(g, carry):
        carry = list(carry)
        packed_low = north_recv[g]
        packed_high = south_recv[g]
        for l in range(GROUP):
            k = g * GROUP + l
            mid = (k.astype(jnp.float32) + 0.5) * (1.0 / K)
            velx[k, 7:8, :] = east_recv[g, 7 * l + 6 : 7 * l + 7, :]
            low = roll(packed_low, 120 - 16 * l, 1)
            high = roll(packed_high, -16 * l, 1)
            vy = vely[k]
            we, ae = face(mid, east_limit, velx[k, 8:24, :] + east_speed)
            ww, aw = face(mid, west_limit, velx[k, 7:23, :] + west_speed)
            wn, an = face(mid, north_limit, vy + north_speed)
            ws, as_ = face(
                mid, south_limit, jnp.where(lane == 0, roll(low, 7, 1), roll(vy, 1, 1)) + south_speed
            )
            inv = inverse[k]
            low_gain = lower[k]
            for t in range(2):
                text[t, k, 5:8, :] = east_recv[g, 7 * l + 3 * t : 7 * l + 3 * t + 3, :]
                text[t, k, 24:27, :] = west_recv[g, 6 * l + 3 * t : 6 * l + 3 * t + 3, :]
                cells = [text[t, k, 8 + s : 24 + s, :] for s in range(-3, 4)]
                center = cells[3]
                change = flux(cells[1:], we, ae) - flux(cells[:6], ww, aw)
                below = low if t == 0 else roll(low, 3, 1)
                above = high if t == 0 else roll(high, -3, 1)
                cells = (
                    [roll(jnp.where(lane >= CY - s, below, center), s, 1) for s in (3, 2, 1)]
                    + [center]
                    + [roll(jnp.where(lane < s, above, center), -s, 1) for s in (1, 2, 3)]
                )
                change = change + (flux(cells[1:], wn, an) - flux(cells[:6], ws, as_))
                carry[t] = (center - change) * inv + low_gain * carry[t]
                values[t, k] = carry[t]
        return tuple(carry)

    carry = (zero, zero)
    for chunk in range(CHUNKS):
        for direction in range(2):
            copy, dst, part, dx = x_copy(direction, chunk)
            pl.when(has(-dx, 0))(copy.wait_recv)
        carry = lax.fori_loop(chunk * CHUNK, chunk * CHUNK + CHUNK, advance, carry)

    def out_copy(chunk):
        part = pl.ds(chunk * CHUNK * GROUP, CHUNK * GROUP)
        return pltpu.make_async_copy(values.at[:, part], tracers_out.at[:, part], out_sem.at[chunk])

    def back(index, carry):
        k = K - 1 - index
        g = gain[k]
        result = tuple(values[t, k] + g * carry[t] for t in range(2))
        for t in range(2):
            values[t, k] = result[t]
        return result

    carry = (zero, zero)
    for chunk in range(CHUNKS - 1, -1, -1):
        first = (CHUNKS - 1 - chunk) * CHUNK * GROUP
        carry = lax.fori_loop(first, first + CHUNK * GROUP, back, carry, unroll=4)
        out_copy(chunk).start()
    for chunk in range(CHUNKS):
        out_copy(chunk).wait()

    for index, (dx, dy) in enumerate(DIRECTIONS):
        pl.when(has(dx, dy))(barotropic_copy(index)[0].wait_send)
    for direction in range(2):
        copy, _, dy = y_copy(direction)
        pl.when(has(0, dy))(copy.wait_send)
        for chunk in range(CHUNKS):
            copy, _, _, dx = x_copy(direction, chunk)
            pl.when(has(dx, 0))(copy.wait_send)


def per_device(nx, ny, tracers, velocity, mixing, levels, surface, transport, forcing):
    f32 = jnp.float32
    anywhere = pl.BlockSpec(memory_space=pl.ANY)
    vmem = pl.BlockSpec(memory_space=pltpu.VMEM)
    return pl.pallas_call(
        functools.partial(kernel, nx, ny),
        out_shape=(
            jax.ShapeDtypeStruct((CX, CY), f32),
            jax.ShapeDtypeStruct((2, CX, CY), f32),
            jax.ShapeDtypeStruct((2, CX, CY), f32),
            jax.ShapeDtypeStruct((2, K, CX, CY), f32),
        ),
        in_specs=[anywhere] * 7,
        out_specs=(vmem, vmem, vmem, anywhere),
        scratch_shapes=[
            pltpu.VMEM((6, ROWS, CY), f32),
            pltpu.VMEM((2, CX, CY), f32),
            pltpu.VMEM((2, CX, CY), f32),
            pltpu.VMEM((2, ROWS, CY), f32),
            pltpu.VMEM((2, ROWS, CY), f32),
            pltpu.VMEM((CX, CY), jnp.int32),
            pltpu.VMEM((2, K, 32, CY), f32),
            pltpu.VMEM((K, 24, CY), f32),
            pltpu.VMEM((K, CX, CY), f32),
            pltpu.VMEM((K, CX, CY), f32),
            pltpu.VMEM((K, CX, CY), f32),
            pltpu.VMEM((K, CX, CY), f32),
            pltpu.VMEM((K, CX, CY), f32),
            pltpu.VMEM((2, K, CX, CY), f32),
            pltpu.VMEM((GROUPS, EAST_ROWS, CY), f32),
            pltpu.VMEM((GROUPS, WEST_ROWS, CY), f32),
            pltpu.VMEM((GROUPS, EAST_ROWS, CY), f32),
            pltpu.VMEM((GROUPS, WEST_ROWS, CY), f32),
            pltpu.VMEM((GROUPS, CX, CY), f32),
            pltpu.VMEM((GROUPS, CX, CY), f32),
            pltpu.VMEM((GROUPS, CX, CY), f32),
            pltpu.VMEM((GROUPS, CX, CY), f32),
            pltpu.VMEM((6, 2, ROWS, CY), f32),
            pltpu.VMEM((5, 2, ROWS, CY), f32),
            pltpu.SemaphoreType.DMA((8,)),
            pltpu.SemaphoreType.DMA((CHUNKS,)),
            pltpu.SemaphoreType.DMA((len(DIRECTIONS),)),
            pltpu.SemaphoreType.DMA((len(DIRECTIONS),)),
            pltpu.SemaphoreType.DMA((2, CHUNKS)),
            pltpu.SemaphoreType.DMA((2, CHUNKS)),
            pltpu.SemaphoreType.DMA((2,)),
            pltpu.SemaphoreType.DMA((2,)),
        ],
        compiler_params=pltpu.CompilerParams(
            collective_id=0, has_side_effects=True, vmem_limit_bytes=40 * 1024 * 1024
        ),
    )(tracers, velocity, mixing, levels, surface, transport, forcing)


def solution(mesh):
    placed = (
        P(None, None, "gx", "gy"),
        P(None, None, "gx", "gy"),
        P(None, "gx", "gy"),
        P("gx", "gy"),
        P("gx", "gy"),
        P(None, "gx", "gy"),
        P(None, "gx", "gy"),
    )
    return jax.shard_map(
        functools.partial(per_device, mesh.shape["gx"], mesh.shape["gy"]),
        mesh=mesh,
        in_specs=placed,
        out_specs=(
            P("gx", "gy"),
            P(None, "gx", "gy"),
            P(None, "gx", "gy"),
            P(None, None, "gx", "gy"),
        ),
        check_vma=False,
    )
```

```python
import functools

import jax
import jax.numpy as jnp
from jax import lax
from jax.experimental import pallas as pl
from jax.experimental.pallas import tpu as pltpu
from jax.sharding import PartitionSpec as P

K = 80
STEPS = 24
CX = 16
CY = 128
GROUP = 8
GROUPS = K // GROUP
CHUNKS = 5
CHUNK = GROUPS // CHUNKS
ROWS = 72
VMEM = 60 * 1024 * 1024
OWN = 32
EAST_ROWS = 7 * GROUP
WEST_ROWS = 6 * GROUP
MESH = pl.DeviceIdType.MESH

DIRECTIONS = [(dx, dy) for dx in (1, -1, 2, -2, 0) for dy in (0, 1, -1) if (dx, dy) != (0, 0)]


def roll(x, shift, axis):
    return pltpu.roll(x, shift % x.shape[axis], axis)


def kernel(
    nx, ny,
    tracers, velocity, mixing, levels, surface, transport, forcing,
    surface_out, transport_out, mean_out, values_out, gain_out,
    fields, pack_w, pack_e, halo_e, halo_w, lev,
    text, velx, vely, mix, lower, inverse, values, gain, mean,
    east_send, west_send, east_recv, west_recv,
    north_send, south_send, north_recv, south_recv,
    coef, state,
    local_sem, out_sem, b_send, b_recv, x_send, x_recv, y_send, y_recv,
):
    gx = lax.axis_index("gx")
    gy = lax.axis_index("gy")

    def has(dx, dy):
        x, y = gx + dx, gy + dy
        return (x >= 0) & (x < nx) & (y >= 0) & (y < ny)

    def device(dx, dy):
        return (lax.rem(gx + dx + nx, nx), lax.rem(gy + dy + ny, ny))

    own = pl.ds(OWN, CX)
    loads = [
        pltpu.make_async_copy(surface, fields.at[0, own, :], local_sem.at[0]),
        pltpu.make_async_copy(transport, fields.at[1:3, own, :], local_sem.at[1]),
        pltpu.make_async_copy(forcing, fields.at[3:5, own, :], local_sem.at[2]),
        pltpu.make_async_copy(levels, lev, local_sem.at[3]),
        pltpu.make_async_copy(tracers, text.at[:, :, 8:24, :], local_sem.at[4]),
        pltpu.make_async_copy(velocity.at[0], velx.at[:, 8:24, :], local_sem.at[5]),
        pltpu.make_async_copy(velocity.at[1], vely, local_sem.at[6]),
        pltpu.make_async_copy(mixing, mix.at[0 : K - 1], local_sem.at[7]),
    ]
    for load in loads:
        load.start()

    barrier = pltpu.get_barrier_semaphore()
    count = jnp.int32(0)
    for dx, dy in DIRECTIONS:
        there = has(dx, dy)

        @pl.when(there)
        def _():
            pl.semaphore_signal(barrier, inc=1, device_id=device(dx, dy), device_id_type=MESH)

        count = count + there.astype(jnp.int32)

    lane = lax.broadcasted_iota(jnp.int32, (CX, CY), 1)

    for load in loads[:4]:
        load.wait()
    fields[5, OWN : OWN + CX, :] = lev[...].astype(jnp.float32) * (1.0 / K)
    for group in range(2):
        east = None
        west = None
        for slot in range(4 if group == 0 else 2):
            x = fields[4 * group + slot, OWN : OWN + CX, :]
            inside = (lane >= 32 * slot) & (lane < 32 * slot + 32)
            to_east = roll(x, 32 * slot + 32, 1)
            to_west = roll(x, 32 * slot, 1)
            east = to_east if east is None else jnp.where(inside, to_east, east)
            west = to_west if west is None else jnp.where(inside, to_west, west)
        pack_e[group] = east
        pack_w[group] = west

    def barotropic_copy(index):
        dx, dy = DIRECTIONS[index]
        rows = 8 if dx == -2 else CX
        start = CX * (2 - dx)
        if dy == 0:
            src, dst = fields.at[:, pl.ds(OWN, rows), :], fields
        elif dy == 1:
            src, dst = pack_e.at[:, pl.ds(0, rows), :], halo_w
        else:
            src, dst = pack_w.at[:, pl.ds(0, rows), :], halo_e
        return (
            pltpu.make_async_remote_copy(
                src_ref=src,
                dst_ref=dst.at[:, pl.ds(start, rows), :],
                send_sem=b_send.at[index],
                recv_sem=b_recv.at[index],
                device_id=device(dx, dy),
                device_id_type=MESH,
            ),
            dst,
            start,
            rows,
        )

    def x_copy(direction, chunk):
        src, dst, dx = ((east_send, east_recv, 1), (west_send, west_recv, -1))[direction]
        part = pl.ds(chunk * CHUNK, CHUNK)
        return pltpu.make_async_remote_copy(
            src_ref=src.at[part], dst_ref=dst.at[part],
            send_sem=x_send.at[direction, chunk], recv_sem=x_recv.at[direction, chunk],
            device_id=device(dx, 0), device_id_type=MESH,
        ), dst, part, dx

    def y_copy(direction):
        src, dst, dy = ((north_send, north_recv, 1), (south_send, south_recv, -1))[direction]
        return pltpu.make_async_remote_copy(
            src_ref=src, dst_ref=dst,
            send_sem=y_send.at[direction], recv_sem=y_recv.at[direction],
            device_id=device(0, dy), device_id_type=MESH,
        ), dst, dy

    pl.semaphore_wait(barrier, count)
    for index, (dx, dy) in enumerate(DIRECTIONS):
        copy, dst, start, rows = barotropic_copy(index)
        pl.when(has(dx, dy))(copy.start)

        @pl.when(jnp.logical_not(has(-dx, -dy)))
        def _():
            dst[:, pl.ds(start, rows), :] = jnp.zeros((dst.shape[0], rows, CY), jnp.float32)

    for load in loads[4:7]:
        load.wait()

    def pack_x(g, carry):
        for l in range(GROUP):
            k = g * GROUP + l
            for t in range(2):
                east_send[g, 7 * l + 3 * t : 7 * l + 3 * t + 3, :] = text[t, k, 21:24, :]
                west_send[g, 6 * l + 3 * t : 6 * l + 3 * t + 3, :] = text[t, k, 8:11, :]
            east_send[g, 7 * l + 6 : 7 * l + 7, :] = velx[k, 23:24, :]
        return carry

    for chunk in range(CHUNKS):
        lax.fori_loop(chunk * CHUNK, chunk * CHUNK + CHUNK, pack_x, 0)
        for direction in range(2):
            copy, dst, part, dx = x_copy(direction, chunk)
            pl.when(has(dx, 0))(copy.start)

            @pl.when(jnp.logical_not(has(-dx, 0)))
            def _():
                dst[part] = jnp.zeros((CHUNK,) + dst.shape[1:], jnp.float32)

    def pack_y(g, carry):
        north = jnp.zeros((CX, CY), jnp.float32)
        south = jnp.zeros((CX, CY), jnp.float32)
        for l in range(GROUP):
            k = g * GROUP + l
            t0 = text[0, k, 8:24, :]
            t1 = text[1, k, 8:24, :]
            high = jnp.where(
                lane >= 125, t0,
                jnp.where(lane >= 122, roll(t1, -3, 1), jnp.where(lane == 121, roll(vely[k], -6, 1), 0.0)),
            )
            low = jnp.where(lane < 3, t0, jnp.where(lane < 6, roll(t1, 3, 1), 0.0))
            north = north + roll(high, 16 * l + 8, 1)
            south = south + roll(low, 16 * l, 1)
        north_send[g] = north
        south_send[g] = south
        return carry

    lax.fori_loop(0, GROUPS, pack_y, 0)
    for direction in range(2):
        copy, dst, dy = y_copy(direction)
        pl.when(has(0, dy))(copy.start)

        @pl.when(jnp.logical_not(has(0, -dy)))
        def _():
            dst[...] = jnp.zeros(dst.shape, jnp.float32)

    loads[7].wait()
    mix[K - 1] = jnp.zeros((CX, CY), jnp.float32)

    def factor(k, carry):
        below, previous = carry
        upper = jnp.where(k + 1 < lev[...], mix[k], 0.0)
        inv = 1.0 / (1.0 + below + upper - below * previous)
        g = upper * inv
        gain[k] = g
        inverse[k] = inv
        lower[k] = below * inv
        return upper, g

    zero = jnp.zeros((CX, CY), jnp.float32)
    lax.fori_loop(0, K, factor, (zero, zero), unroll=4)
    own_state = pl.ds(OWN, CX)
    stores = [
        pltpu.make_async_copy(gain, gain_out, out_sem.at[CHUNKS]),
        pltpu.make_async_copy(state.at[0, 0, own_state, :], surface_out, out_sem.at[CHUNKS + 1]),
        pltpu.make_async_copy(state.at[1:3, 0, own_state, :], transport_out, out_sem.at[CHUNKS + 2]),
        pltpu.make_async_copy(mean, mean_out, out_sem.at[CHUNKS + 3]),
    ]
    stores[0].start()

    for index, (dx, dy) in enumerate(DIRECTIONS):
        copy = barotropic_copy(index)[0]
        pl.when(has(-dx, -dy))(copy.wait_recv)

    wide = lax.broadcasted_iota(jnp.int32, (ROWS, CY), 1)

    def beside(index):
        group, slot = divmod(index, 4)
        return jnp.where(
            wide < 64, roll(halo_e[group], -32 * slot, 1), roll(halo_w[group], 96 - 32 * slot, 1)
        )

    def upper_x(pair):
        return tuple(roll(x, -1, 0) for x in pair)

    def lower_x(pair):
        return tuple(roll(x, 1, 0) for x in pair)

    def upper_y(pair):
        a, b = (roll(x, -1, 1) for x in pair)
        return jnp.where(wide == CY - 1, b, a), jnp.where(wide == CY - 1, a, b)

    def lower_y(pair):
        a, b = (roll(x, 1, 1) for x in pair)
        return jnp.where(wide == 0, b, a), jnp.where(wide == 0, a, b)

    depth = (fields[5], beside(5))
    east_depth = tuple(jnp.minimum(a, b) for a, b in zip(depth, upper_x(depth)))
    north_depth = tuple(jnp.minimum(a, b) for a, b in zip(depth, upper_y(depth)))
    for tile in range(2):
        other = (lambda i: fields[i]) if tile == 0 else beside
        coef[0, tile] = 0.9 * east_depth[tile]
        coef[1, tile] = 0.5 * east_depth[tile] * other(3)
        coef[2, tile] = 0.9 * north_depth[tile]
        coef[3, tile] = 0.5 * north_depth[tile] * other(4)
        coef[4, tile] = east_depth[tile]
        coef[5, tile] = north_depth[tile]
        state[0, tile] = other(0)
        state[1, tile] = jnp.where(east_depth[tile] > 0.0, other(1), 0.0)
        state[2, tile] = jnp.where(north_depth[tile] > 0.0, other(2), 0.0)
        state[3, tile] = jnp.zeros((ROWS, CY), jnp.float32)
        state[4, tile] = jnp.zeros((ROWS, CY), jnp.float32)

    def substep(step, carry):
        east = (state[1, 0], state[1, 1])
        north = (state[2, 0], state[2, 1])
        east_low = lower_x(east)
        north_low = lower_y(north)
        height = tuple(
            state[0, i] - 0.5 * ((east[i] - east_low[i]) + (north[i] - north_low[i])) for i in range(2)
        )
        high_x = upper_x(height)
        high_y = upper_y(height)
        for i in range(2):
            state[0, i] = height[i]
            e = east[i] - coef[0, i] * (high_x[i] - height[i]) + coef[1, i]
            n = north[i] - coef[2, i] * (high_y[i] - height[i]) + coef[3, i]
            state[1, i] = e
            state[2, i] = n
            state[3, i] = state[3, i] + e
            state[4, i] = state[4, i] + n
        return carry

    lax.fori_loop(0, STEPS, substep, 0)

    mean[0] = state[3, 0, OWN : OWN + CX, :] * (1.0 / STEPS)
    mean[1] = state[4, 0, OWN : OWN + CX, :] * (1.0 / STEPS)
    for store in stores[1:]:
        store.start()

    scale = 0.01 / STEPS
    for i in range(2):
        state[3, i] = scale * state[3, i] / jnp.maximum(coef[4, i], 1.0 / K)
        state[4, i] = scale * state[4, i] / jnp.maximum(coef[5, i], 1.0 / K)

    here = slice(OWN, OWN + CX)
    behind = slice(OWN - 1, OWN + CX - 1)
    east_speed, west_speed = state[3, 0, here, :], state[3, 0, behind, :]
    east_limit, west_limit = coef[4, 0, here, :], coef[4, 0, behind, :]
    north_speed, north_limit = state[4, 0, here, :], coef[5, 0, here, :]
    south_speed = jnp.where(lane == 0, roll(state[4, 1, here, :], 1, 1), roll(north_speed, 1, 1))
    south_limit = jnp.where(lane == 0, roll(coef[5, 1, here, :], 1, 1), roll(north_limit, 1, 1))

    for direction in range(2):
        copy, dst, dy = y_copy(direction)
        pl.when(has(0, -dy))(copy.wait_recv)

    def flux(cells, w, size):
        a, b, c, d, e, f = cells
        even = (a + f) - 8.0 * (b + e) + 37.0 * (c + d)
        odd = (a - f) - 5.0 * (b - e) + 10.0 * (c - d)
        return w * even + size * odd

    def face(mid, limit, value):
        w = jnp.where(mid < limit, value, 0.0) * (1.0 / 60.0)
        return w, jnp.abs(w)

    def advance(g, carry):
        carry = list(carry)
        packed_low = north_recv[g]
        packed_high = south_recv[g]
        for l in range(GROUP):
            k = g * GROUP + l
            mid = (k.astype(jnp.float32) + 0.5) * (1.0 / K)
            velx[k, 7:8, :] = east_recv[g, 7 * l + 6 : 7 * l + 7, :]
            low = roll(packed_low, 120 - 16 * l, 1)
            high = roll(packed_high, -16 * l, 1)
            vy = vely[k]
            we, ae = face(mid, east_limit, velx[k, 8:24, :] + east_speed)
            ww, aw = face(mid, west_limit, velx[k, 7:23, :] + west_speed)
            wn, an = face(mid, north_limit, vy + north_speed)
            ws, as_ = face(
                mid, south_limit, jnp.where(lane == 0, roll(low, 7, 1), roll(vy, 1, 1)) + south_speed
            )
            inv = inverse[k]
            low_gain = lower[k]
            for t in range(2):
                text[t, k, 5:8, :] = east_recv[g, 7 * l + 3 * t : 7 * l + 3 * t + 3, :]
                text[t, k, 24:27, :] = west_recv[g, 6 * l + 3 * t : 6 * l + 3 * t + 3, :]
                cells = [text[t, k, 8 + s : 24 + s, :] for s in range(-3, 4)]
                center = cells[3]
                change = flux(cells[1:], we, ae) - flux(cells[:6], ww, aw)
                below = low if t == 0 else roll(low, 3, 1)
                above = high if t == 0 else roll(high, -3, 1)
                cells = (
                    [roll(jnp.where(lane >= CY - s, below, center), s, 1) for s in (3, 2, 1)]
                    + [center]
                    + [roll(jnp.where(lane < s, above, center), -s, 1) for s in (1, 2, 3)]
                )
                change = change + (flux(cells[1:], wn, an) - flux(cells[:6], ws, as_))
                carry[t] = (center - change) * inv + low_gain * carry[t]
                values[t, k] = carry[t]
        return tuple(carry)

    carry = (zero, zero)
    for chunk in range(CHUNKS):
        for direction in range(2):
            copy, dst, part, dx = x_copy(direction, chunk)
            pl.when(has(-dx, 0))(copy.wait_recv)
        carry = lax.fori_loop(chunk * CHUNK, chunk * CHUNK + CHUNK, advance, carry)
        part = pl.ds(chunk * CHUNK * GROUP, CHUNK * GROUP)
        store = pltpu.make_async_copy(values.at[:, part], values_out.at[:, part], out_sem.at[chunk])
        store.start()
        stores.append(store)
    for store in stores:
        store.wait()

    for index, (dx, dy) in enumerate(DIRECTIONS):
        pl.when(has(dx, dy))(barotropic_copy(index)[0].wait_send)
    for direction in range(2):
        copy, _, dy = y_copy(direction)
        pl.when(has(0, dy))(copy.wait_send)
        for chunk in range(CHUNKS):
            copy, _, _, dx = x_copy(direction, chunk)
            pl.when(has(dx, 0))(copy.wait_send)


def finish(
    surface, transport, mean, values, gain,
    surface_out, transport_out, mean_out, tracers_out,
    held, factor, result, small_sem, in_sem, out_sem,
):
    def part(chunk):
        return pl.ds(chunk * CHUNK * GROUP, CHUNK * GROUP)

    def loads(chunk):
        return (
            pltpu.make_async_copy(gain.at[part(chunk)], factor.at[part(chunk)], in_sem.at[0, chunk]),
            pltpu.make_async_copy(values.at[:, part(chunk)], held.at[:, part(chunk)], in_sem.at[1, chunk]),
        )

    def out_copy(chunk):
        return pltpu.make_async_copy(
            result.at[:, part(chunk)], tracers_out.at[:, part(chunk)], out_sem.at[chunk]
        )

    for chunk in range(CHUNKS - 1, -1, -1):
        for load in loads(chunk):
            load.start()
    small = [
        pltpu.make_async_copy(surface, surface_out, small_sem.at[0]),
        pltpu.make_async_copy(transport, transport_out, small_sem.at[1]),
        pltpu.make_async_copy(mean, mean_out, small_sem.at[2]),
    ]
    for copy in small:
        copy.start()

    def back(index, carry):
        k = K - 1 - index
        g = factor[k]
        now = tuple(held[t, k] + g * carry[t] for t in range(2))
        for t in range(2):
            result[t, k] = now[t]
        return now

    zero = jnp.zeros((CX, CY), jnp.float32)
    carry = (zero, zero)
    for chunk in range(CHUNKS - 1, -1, -1):
        for load in loads(chunk):
            load.wait()
        first = (CHUNKS - 1 - chunk) * CHUNK * GROUP
        carry = lax.fori_loop(first, first + CHUNK * GROUP, back, carry, unroll=8)
        out_copy(chunk).start()
    for copy in small:
        copy.wait()
    for chunk in range(CHUNKS):
        out_copy(chunk).wait()


def per_device(nx, ny, tracers, velocity, mixing, levels, surface, transport, forcing):
    f32 = jnp.float32
    anywhere = pl.BlockSpec(memory_space=pl.ANY)
    held = pl.pallas_call(
        functools.partial(kernel, nx, ny),
        out_shape=(
            jax.ShapeDtypeStruct((CX, CY), f32),
            jax.ShapeDtypeStruct((2, CX, CY), f32),
            jax.ShapeDtypeStruct((2, CX, CY), f32),
            jax.ShapeDtypeStruct((2, K, CX, CY), f32),
            jax.ShapeDtypeStruct((K, CX, CY), f32),
        ),
        in_specs=[anywhere] * 7,
        out_specs=(anywhere,) * 5,
        scratch_shapes=[
            pltpu.VMEM((6, ROWS, CY), f32),
            pltpu.VMEM((2, CX, CY), f32),
            pltpu.VMEM((2, CX, CY), f32),
            pltpu.VMEM((2, ROWS, CY), f32),
            pltpu.VMEM((2, ROWS, CY), f32),
            pltpu.VMEM((CX, CY), jnp.int32),
            pltpu.VMEM((2, K, 32, CY), f32),
            pltpu.VMEM((K, 24, CY), f32),
            pltpu.VMEM((K, CX, CY), f32),
            pltpu.VMEM((K, CX, CY), f32),
            pltpu.VMEM((K, CX, CY), f32),
            pltpu.VMEM((K, CX, CY), f32),
            pltpu.VMEM((2, K, CX, CY), f32),
            pltpu.VMEM((K, CX, CY), f32),
            pltpu.VMEM((2, CX, CY), f32),
            pltpu.VMEM((GROUPS, EAST_ROWS, CY), f32),
            pltpu.VMEM((GROUPS, WEST_ROWS, CY), f32),
            pltpu.VMEM((GROUPS, EAST_ROWS, CY), f32),
            pltpu.VMEM((GROUPS, WEST_ROWS, CY), f32),
            pltpu.VMEM((GROUPS, CX, CY), f32),
            pltpu.VMEM((GROUPS, CX, CY), f32),
            pltpu.VMEM((GROUPS, CX, CY), f32),
            pltpu.VMEM((GROUPS, CX, CY), f32),
            pltpu.VMEM((6, 2, ROWS, CY), f32),
            pltpu.VMEM((5, 2, ROWS, CY), f32),
            pltpu.SemaphoreType.DMA((8,)),
            pltpu.SemaphoreType.DMA((CHUNKS + 4,)),
            pltpu.SemaphoreType.DMA((len(DIRECTIONS),)),
            pltpu.SemaphoreType.DMA((len(DIRECTIONS),)),
            pltpu.SemaphoreType.DMA((2, CHUNKS)),
            pltpu.SemaphoreType.DMA((2, CHUNKS)),
            pltpu.SemaphoreType.DMA((2,)),
            pltpu.SemaphoreType.DMA((2,)),
        ],
        compiler_params=pltpu.CompilerParams(
            collective_id=0, has_side_effects=True, vmem_limit_bytes=VMEM
        ),
    )(tracers, velocity, mixing, levels, surface, transport, forcing)
    return pl.pallas_call(
        finish,
        out_shape=(
            jax.ShapeDtypeStruct((CX, CY), f32),
            jax.ShapeDtypeStruct((2, CX, CY), f32),
            jax.ShapeDtypeStruct((2, CX, CY), f32),
            jax.ShapeDtypeStruct((2, K, CX, CY), f32),
        ),
        in_specs=[anywhere] * 5,
        out_specs=(anywhere,) * 4,
        scratch_shapes=[
            pltpu.VMEM((2, K, CX, CY), f32),
            pltpu.VMEM((K, CX, CY), f32),
            pltpu.VMEM((2, K, CX, CY), f32),
            pltpu.SemaphoreType.DMA((3,)),
            pltpu.SemaphoreType.DMA((2, CHUNKS)),
            pltpu.SemaphoreType.DMA((CHUNKS,)),
        ],
        compiler_params=pltpu.CompilerParams(vmem_limit_bytes=VMEM),
    )(*held)


def solution(mesh):
    placed = (
        P(None, None, "gx", "gy"),
        P(None, None, "gx", "gy"),
        P(None, "gx", "gy"),
        P("gx", "gy"),
        P("gx", "gy"),
        P(None, "gx", "gy"),
        P(None, "gx", "gy"),
    )
    return jax.shard_map(
        functools.partial(per_device, mesh.shape["gx"], mesh.shape["gy"]),
        mesh=mesh,
        in_specs=placed,
        out_specs=(
            P("gx", "gy"),
            P(None, "gx", "gy"),
            P(None, "gx", "gy"),
            P(None, None, "gx", "gy"),
        ),
        check_vma=False,
    )
```

```python
import functools

import jax
import jax.numpy as jnp
from jax import lax
from jax.experimental import pallas as pl
from jax.experimental.pallas import tpu as pltpu
from jax.sharding import PartitionSpec as P

K = 80
STEPS = 24
CX = 16
CY = 128
GROUP = 8
GROUPS = K // GROUP
CHUNKS = 5
CHUNK = GROUPS // CHUNKS
ROWS = 72
VMEM = 60 * 1024 * 1024
OWN = 32
EAST_ROWS = 7 * GROUP
WEST_ROWS = 6 * GROUP
MESH = pl.DeviceIdType.MESH

DIRECTIONS = [(dx, dy) for dx in (1, -1, 2, -2, 0) for dy in (0, 1, -1) if (dx, dy) != (0, 0)]


def roll(x, shift, axis):
    return pltpu.roll(x, shift % x.shape[axis], axis)


def kernel(
    nx, ny,
    tracers, velocity, mixing, levels, surface, transport, forcing,
    surface_out, transport_out, mean_out, values_out, gain_out,
    fields, pack_w, pack_e, halo_e, halo_w, lev,
    text, velx, vely, mix, lower, inverse, values, gain, mean,
    east_send, west_send, east_recv, west_recv,
    north_send, south_send, north_recv, south_recv,
    coef, state,
    local_sem, out_sem, b_send, b_recv, x_send, x_recv, y_send, y_recv,
):
    gx = lax.axis_index("gx")
    gy = lax.axis_index("gy")

    def has(dx, dy):
        x, y = gx + dx, gy + dy
        return (x >= 0) & (x < nx) & (y >= 0) & (y < ny)

    def device(dx, dy):
        return (lax.rem(gx + dx + nx, nx), lax.rem(gy + dy + ny, ny))

    own = pl.ds(OWN, CX)
    loads = [
        pltpu.make_async_copy(surface, fields.at[0, own, :], local_sem.at[0]),
        pltpu.make_async_copy(transport, fields.at[1:3, own, :], local_sem.at[1]),
        pltpu.make_async_copy(forcing, fields.at[3:5, own, :], local_sem.at[2]),
        pltpu.make_async_copy(levels, lev, local_sem.at[3]),
        pltpu.make_async_copy(tracers, text.at[:, :, 8:24, :], local_sem.at[4]),
        pltpu.make_async_copy(velocity.at[0], velx.at[:, 8:24, :], local_sem.at[5]),
        pltpu.make_async_copy(velocity.at[1], vely, local_sem.at[6]),
        pltpu.make_async_copy(mixing, mix.at[0 : K - 1], local_sem.at[7]),
    ]
    for load in loads:
        load.start()

    barrier = pltpu.get_barrier_semaphore()
    count = jnp.int32(0)
    for dx, dy in DIRECTIONS:
        there = has(dx, dy)

        @pl.when(there)
        def _():
            pl.semaphore_signal(barrier, inc=1, device_id=device(dx, dy), device_id_type=MESH)

        count = count + there.astype(jnp.int32)

    lane = lax.broadcasted_iota(jnp.int32, (CX, CY), 1)

    for load in loads[:4]:
        load.wait()
    fields[5, OWN : OWN + CX, :] = lev[...].astype(jnp.float32) * (1.0 / K)
    for group in range(2):
        east = None
        west = None
        for slot in range(4 if group == 0 else 2):
            x = fields[4 * group + slot, OWN : OWN + CX, :]
            inside = (lane >= 32 * slot) & (lane < 32 * slot + 32)
            to_east = roll(x, 32 * slot + 32, 1)
            to_west = roll(x, 32 * slot, 1)
            east = to_east if east is None else jnp.where(inside, to_east, east)
            west = to_west if west is None else jnp.where(inside, to_west, west)
        pack_e[group] = east
        pack_w[group] = west

    def barotropic_copy(index):
        dx, dy = DIRECTIONS[index]
        rows = 8 if dx == -2 else CX
        start = CX * (2 - dx)
        if dy == 0:
            src, dst = fields.at[:, pl.ds(OWN, rows), :], fields
        elif dy == 1:
            src, dst = pack_e.at[:, pl.ds(0, rows), :], halo_w
        else:
            src, dst = pack_w.at[:, pl.ds(0, rows), :], halo_e
        return (
            pltpu.make_async_remote_copy(
                src_ref=src,
                dst_ref=dst.at[:, pl.ds(start, rows), :],
                send_sem=b_send.at[index],
                recv_sem=b_recv.at[index],
                device_id=device(dx, dy),
                device_id_type=MESH,
            ),
            dst,
            start,
            rows,
        )

    def x_copy(direction, chunk):
        src, dst, dx = ((east_send, east_recv, 1), (west_send, west_recv, -1))[direction]
        part = pl.ds(chunk * CHUNK, CHUNK)
        return pltpu.make_async_remote_copy(
            src_ref=src.at[part], dst_ref=dst.at[part],
            send_sem=x_send.at[direction, chunk], recv_sem=x_recv.at[direction, chunk],
            device_id=device(dx, 0), device_id_type=MESH,
        ), dst, part, dx

    def y_copy(direction):
        src, dst, dy = ((north_send, north_recv, 1), (south_send, south_recv, -1))[direction]
        return pltpu.make_async_remote_copy(
            src_ref=src, dst_ref=dst,
            send_sem=y_send.at[direction], recv_sem=y_recv.at[direction],
            device_id=device(0, dy), device_id_type=MESH,
        ), dst, dy

    pl.semaphore_wait(barrier, count)
    for index, (dx, dy) in enumerate(DIRECTIONS):
        copy, dst, start, rows = barotropic_copy(index)
        pl.when(has(dx, dy))(copy.start)

        @pl.when(jnp.logical_not(has(-dx, -dy)))
        def _():
            dst[:, pl.ds(start, rows), :] = jnp.zeros((dst.shape[0], rows, CY), jnp.float32)

    for load in loads[4:7]:
        load.wait()

    def pack_x(g, carry):
        for l in range(GROUP):
            k = g * GROUP + l
            for t in range(2):
                east_send[g, 7 * l + 3 * t : 7 * l + 3 * t + 3, :] = text[t, k, 21:24, :]
                west_send[g, 6 * l + 3 * t : 6 * l + 3 * t + 3, :] = text[t, k, 8:11, :]
            east_send[g, 7 * l + 6 : 7 * l + 7, :] = velx[k, 23:24, :]
        return carry

    for chunk in range(CHUNKS):
        lax.fori_loop(chunk * CHUNK, chunk * CHUNK + CHUNK, pack_x, 0)
        for direction in range(2):
            copy, dst, part, dx = x_copy(direction, chunk)
            pl.when(has(dx, 0))(copy.start)

            @pl.when(jnp.logical_not(has(-dx, 0)))
            def _():
                dst[part] = jnp.zeros((CHUNK,) + dst.shape[1:], jnp.float32)

    def pack_y(g, carry):
        north = jnp.zeros((CX, CY), jnp.float32)
        south = jnp.zeros((CX, CY), jnp.float32)
        for l in range(GROUP):
            k = g * GROUP + l
            t0 = text[0, k, 8:24, :]
            t1 = text[1, k, 8:24, :]
            high = jnp.where(
                lane >= 125, t0,
                jnp.where(lane >= 122, roll(t1, -3, 1), jnp.where(lane == 121, roll(vely[k], -6, 1), 0.0)),
            )
            low = jnp.where(lane < 3, t0, jnp.where(lane < 6, roll(t1, 3, 1), 0.0))
            north = north + roll(high, 16 * l + 8, 1)
            south = south + roll(low, 16 * l, 1)
        north_send[g] = north
        south_send[g] = south
        return carry

    lax.fori_loop(0, GROUPS, pack_y, 0)
    for direction in range(2):
        copy, dst, dy = y_copy(direction)
        pl.when(has(0, dy))(copy.start)

        @pl.when(jnp.logical_not(has(0, -dy)))
        def _():
            dst[...] = jnp.zeros(dst.shape, jnp.float32)

    loads[7].wait()
    mix[K - 1] = jnp.zeros((CX, CY), jnp.float32)

    def factor(k, carry):
        below, previous = carry
        upper = jnp.where(k + 1 < lev[...], mix[k], 0.0)
        inv = 1.0 / (1.0 + below + upper - below * previous)
        g = upper * inv
        gain[k] = g
        inverse[k] = inv
        lower[k] = below * inv
        return upper, g

    zero = jnp.zeros((CX, CY), jnp.float32)
    own_state = pl.ds(OWN, CX)
    stores = [
        pltpu.make_async_copy(gain, gain_out, out_sem.at[CHUNKS]),
        pltpu.make_async_copy(state.at[0, 0, own_state, :], surface_out, out_sem.at[CHUNKS + 1]),
        pltpu.make_async_copy(state.at[1:3, 0, own_state, :], transport_out, out_sem.at[CHUNKS + 2]),
        pltpu.make_async_copy(mean, mean_out, out_sem.at[CHUNKS + 3]),
    ]

    for index, (dx, dy) in enumerate(DIRECTIONS):
        copy = barotropic_copy(index)[0]
        pl.when(has(-dx, -dy))(copy.wait_recv)

    wide = lax.broadcasted_iota(jnp.int32, (ROWS, CY), 1)

    def beside(index):
        group, slot = divmod(index, 4)
        return jnp.where(
            wide < 64, roll(halo_e[group], -32 * slot, 1), roll(halo_w[group], 96 - 32 * slot, 1)
        )

    def upper_x(pair):
        return tuple(roll(x, -1, 0) for x in pair)

    def lower_x(pair):
        return tuple(roll(x, 1, 0) for x in pair)

    def upper_y(pair):
        a, b = (roll(x, -1, 1) for x in pair)
        last = wide[: a.shape[0]] == CY - 1
        return jnp.where(last, b, a), jnp.where(last, a, b)

    def lower_y(pair):
        a, b = (roll(x, 1, 1) for x in pair)
        first = wide[: a.shape[0]] == 0
        return jnp.where(first, b, a), jnp.where(first, a, b)

    depth = (fields[5], beside(5))
    east_depth = tuple(jnp.minimum(a, b) for a, b in zip(depth, upper_x(depth)))
    north_depth = tuple(jnp.minimum(a, b) for a, b in zip(depth, upper_y(depth)))
    for tile in range(2):
        other = (lambda i: fields[i]) if tile == 0 else beside
        coef[0, tile] = 0.9 * east_depth[tile]
        coef[1, tile] = 0.5 * east_depth[tile] * other(3)
        coef[2, tile] = 0.9 * north_depth[tile]
        coef[3, tile] = 0.5 * north_depth[tile] * other(4)
        coef[4, tile] = east_depth[tile]
        coef[5, tile] = north_depth[tile]
        state[0, tile] = other(0)
        state[1, tile] = jnp.where(east_depth[tile] > 0.0, other(1), 0.0)
        state[2, tile] = jnp.where(north_depth[tile] > 0.0, other(2), 0.0)
        state[3, tile] = jnp.zeros((ROWS, CY), jnp.float32)
        state[4, tile] = jnp.zeros((ROWS, CY), jnp.float32)

    def substep(low, high, levels_each, first_step, first_level, step, carry):
        for extra in range(levels_each):
            carry = factor(first_level + (step - first_step) * levels_each + extra, carry)
        rows = slice(low, high)
        east = (state[1, 0, rows, :], state[1, 1, rows, :])
        north = (state[2, 0, rows, :], state[2, 1, rows, :])
        east_low = lower_x(east)
        north_low = lower_y(north)
        height = tuple(
            state[0, i, rows, :] - 0.5 * ((east[i] - east_low[i]) + (north[i] - north_low[i]))
            for i in range(2)
        )
        high_x = upper_x(height)
        high_y = upper_y(height)
        for i in range(2):
            state[0, i, rows, :] = height[i]
            e = east[i] - coef[0, i, rows, :] * (high_x[i] - height[i]) + coef[1, i, rows, :]
            n = north[i] - coef[2, i, rows, :] * (high_y[i] - height[i]) + coef[3, i, rows, :]
            state[1, i, rows, :] = e
            state[2, i, rows, :] = n
            state[3, i, rows, :] = state[3, i, rows, :] + e
            state[4, i, rows, :] = state[4, i, rows, :] + n
        return carry

    factors = (zero, zero)
    for low, high, levels_each, first_step, first_level in (
        (0, 72, 4, 0, 0), (8, 64, 4, 8, 32), (16, 56, 2, 16, 64),
    ):
        factors = lax.fori_loop(
            first_step, first_step + 8,
            functools.partial(substep, low, high, levels_each, first_step, first_level), factors,
        )
    stores[0].start()

    mean[0] = state[3, 0, OWN : OWN + CX, :] * (1.0 / STEPS)
    mean[1] = state[4, 0, OWN : OWN + CX, :] * (1.0 / STEPS)
    for store in stores[1:]:
        store.start()

    scale = 0.01 / STEPS
    for i in range(2):
        state[3, i] = scale * state[3, i] / jnp.maximum(coef[4, i], 1.0 / K)
        state[4, i] = scale * state[4, i] / jnp.maximum(coef[5, i], 1.0 / K)

    here = slice(OWN, OWN + CX)
    behind = slice(OWN - 1, OWN + CX - 1)
    east_speed, west_speed = state[3, 0, here, :], state[3, 0, behind, :]
    east_limit, west_limit = coef[4, 0, here, :], coef[4, 0, behind, :]
    north_speed, north_limit = state[4, 0, here, :], coef[5, 0, here, :]
    south_speed = jnp.where(lane == 0, roll(state[4, 1, here, :], 1, 1), roll(north_speed, 1, 1))
    south_limit = jnp.where(lane == 0, roll(coef[5, 1, here, :], 1, 1), roll(north_limit, 1, 1))

    for direction in range(2):
        copy, dst, dy = y_copy(direction)
        pl.when(has(0, -dy))(copy.wait_recv)

    def flux(cells, w, size):
        a, b, c, d, e, f = cells
        even = (a + f) - 8.0 * (b + e) + 37.0 * (c + d)
        odd = (a - f) - 5.0 * (b - e) + 10.0 * (c - d)
        return w * even + size * odd

    def face(mid, limit, value):
        w = jnp.where(mid < limit, value, 0.0) * (1.0 / 60.0)
        return w, jnp.abs(w)

    def advance(g, carry):
        carry = list(carry)
        packed_low = north_recv[g]
        packed_high = south_recv[g]
        for l in range(GROUP):
            k = g * GROUP + l
            mid = (k.astype(jnp.float32) + 0.5) * (1.0 / K)
            velx[k, 7:8, :] = east_recv[g, 7 * l + 6 : 7 * l + 7, :]
            low = roll(packed_low, 120 - 16 * l, 1)
            high = roll(packed_high, -16 * l, 1)
            vy = vely[k]
            we, ae = face(mid, east_limit, velx[k, 8:24, :] + east_speed)
            ww, aw = face(mid, west_limit, velx[k, 7:23, :] + west_speed)
            wn, an = face(mid, north_limit, vy + north_speed)
            ws, as_ = face(
                mid, south_limit, jnp.where(lane == 0, roll(low, 7, 1), roll(vy, 1, 1)) + south_speed
            )
            inv = inverse[k]
            low_gain = lower[k]
            for t in range(2):
                text[t, k, 5:8, :] = east_recv[g, 7 * l + 3 * t : 7 * l + 3 * t + 3, :]
                text[t, k, 24:27, :] = west_recv[g, 6 * l + 3 * t : 6 * l + 3 * t + 3, :]
                cells = [text[t, k, 8 + s : 24 + s, :] for s in range(-3, 4)]
                center = cells[3]
                change = flux(cells[1:], we, ae) - flux(cells[:6], ww, aw)
                below = low if t == 0 else roll(low, 3, 1)
                above = high if t == 0 else roll(high, -3, 1)
                cells = (
                    [roll(jnp.where(lane >= CY - s, below, center), s, 1) for s in (3, 2, 1)]
                    + [center]
                    + [roll(jnp.where(lane < s, above, center), -s, 1) for s in (1, 2, 3)]
                )
                change = change + (flux(cells[1:], wn, an) - flux(cells[:6], ws, as_))
                carry[t] = (center - change) * inv + low_gain * carry[t]
                values[t, k] = carry[t]
        return tuple(carry)

    carry = (zero, zero)
    for chunk in range(CHUNKS):
        for direction in range(2):
            copy, dst, part, dx = x_copy(direction, chunk)
            pl.when(has(-dx, 0))(copy.wait_recv)
        carry = lax.fori_loop(chunk * CHUNK, chunk * CHUNK + CHUNK, advance, carry)
        part = pl.ds(chunk * CHUNK * GROUP, CHUNK * GROUP)
        store = pltpu.make_async_copy(values.at[:, part], values_out.at[:, part], out_sem.at[chunk])
        store.start()
        stores.append(store)
    for store in stores:
        store.wait()

    for index, (dx, dy) in enumerate(DIRECTIONS):
        pl.when(has(dx, dy))(barotropic_copy(index)[0].wait_send)
    for direction in range(2):
        copy, _, dy = y_copy(direction)
        pl.when(has(0, dy))(copy.wait_send)
        for chunk in range(CHUNKS):
            copy, _, _, dx = x_copy(direction, chunk)
            pl.when(has(dx, 0))(copy.wait_send)


def finish(
    surface, transport, mean, values, gain,
    surface_out, transport_out, mean_out, tracers_out,
    held, factor, result, small_sem, in_sem, out_sem,
):
    def part(chunk):
        return pl.ds(chunk * CHUNK * GROUP, CHUNK * GROUP)

    def loads(chunk):
        return (
            pltpu.make_async_copy(gain.at[part(chunk)], factor.at[part(chunk)], in_sem.at[0, chunk]),
            pltpu.make_async_copy(values.at[:, part(chunk)], held.at[:, part(chunk)], in_sem.at[1, chunk]),
        )

    def out_copy(chunk):
        return pltpu.make_async_copy(
            result.at[:, part(chunk)], tracers_out.at[:, part(chunk)], out_sem.at[chunk]
        )

    for chunk in range(CHUNKS - 1, -1, -1):
        for load in loads(chunk):
            load.start()
    small = [
        pltpu.make_async_copy(surface, surface_out, small_sem.at[0]),
        pltpu.make_async_copy(transport, transport_out, small_sem.at[1]),
        pltpu.make_async_copy(mean, mean_out, small_sem.at[2]),
    ]
    for copy in small:
        copy.start()

    def back(index, carry):
        k = K - 1 - index
        g = factor[k]
        now = tuple(held[t, k] + g * carry[t] for t in range(2))
        for t in range(2):
            result[t, k] = now[t]
        return now

    zero = jnp.zeros((CX, CY), jnp.float32)
    carry = (zero, zero)
    for chunk in range(CHUNKS - 1, -1, -1):
        for load in loads(chunk):
            load.wait()
        first = (CHUNKS - 1 - chunk) * CHUNK * GROUP
        carry = lax.fori_loop(first, first + CHUNK * GROUP, back, carry, unroll=8)
        out_copy(chunk).start()
    for copy in small:
        copy.wait()
    for chunk in range(CHUNKS):
        out_copy(chunk).wait()


def per_device(nx, ny, tracers, velocity, mixing, levels, surface, transport, forcing):
    f32 = jnp.float32
    anywhere = pl.BlockSpec(memory_space=pl.ANY)
    held = pl.pallas_call(
        functools.partial(kernel, nx, ny),
        out_shape=(
            jax.ShapeDtypeStruct((CX, CY), f32),
            jax.ShapeDtypeStruct((2, CX, CY), f32),
            jax.ShapeDtypeStruct((2, CX, CY), f32),
            jax.ShapeDtypeStruct((2, K, CX, CY), f32),
            jax.ShapeDtypeStruct((K, CX, CY), f32),
        ),
        in_specs=[anywhere] * 7,
        out_specs=(anywhere,) * 5,
        scratch_shapes=[
            pltpu.VMEM((6, ROWS, CY), f32),
            pltpu.VMEM((2, CX, CY), f32),
            pltpu.VMEM((2, CX, CY), f32),
            pltpu.VMEM((2, ROWS, CY), f32),
            pltpu.VMEM((2, ROWS, CY), f32),
            pltpu.VMEM((CX, CY), jnp.int32),
            pltpu.VMEM((2, K, 32, CY), f32),
            pltpu.VMEM((K, 24, CY), f32),
            pltpu.VMEM((K, CX, CY), f32),
            pltpu.VMEM((K, CX, CY), f32),
            pltpu.VMEM((K, CX, CY), f32),
            pltpu.VMEM((K, CX, CY), f32),
            pltpu.VMEM((2, K, CX, CY), f32),
            pltpu.VMEM((K, CX, CY), f32),
            pltpu.VMEM((2, CX, CY), f32),
            pltpu.VMEM((GROUPS, EAST_ROWS, CY), f32),
            pltpu.VMEM((GROUPS, WEST_ROWS, CY), f32),
            pltpu.VMEM((GROUPS, EAST_ROWS, CY), f32),
            pltpu.VMEM((GROUPS, WEST_ROWS, CY), f32),
            pltpu.VMEM((GROUPS, CX, CY), f32),
            pltpu.VMEM((GROUPS, CX, CY), f32),
            pltpu.VMEM((GROUPS, CX, CY), f32),
            pltpu.VMEM((GROUPS, CX, CY), f32),
            pltpu.VMEM((6, 2, ROWS, CY), f32),
            pltpu.VMEM((5, 2, ROWS, CY), f32),
            pltpu.SemaphoreType.DMA((8,)),
            pltpu.SemaphoreType.DMA((CHUNKS + 4,)),
            pltpu.SemaphoreType.DMA((len(DIRECTIONS),)),
            pltpu.SemaphoreType.DMA((len(DIRECTIONS),)),
            pltpu.SemaphoreType.DMA((2, CHUNKS)),
            pltpu.SemaphoreType.DMA((2, CHUNKS)),
            pltpu.SemaphoreType.DMA((2,)),
            pltpu.SemaphoreType.DMA((2,)),
        ],
        compiler_params=pltpu.CompilerParams(
            collective_id=0, has_side_effects=True, vmem_limit_bytes=VMEM
        ),
    )(tracers, velocity, mixing, levels, surface, transport, forcing)
    return pl.pallas_call(
        finish,
        out_shape=(
            jax.ShapeDtypeStruct((CX, CY), f32),
            jax.ShapeDtypeStruct((2, CX, CY), f32),
            jax.ShapeDtypeStruct((2, CX, CY), f32),
            jax.ShapeDtypeStruct((2, K, CX, CY), f32),
        ),
        in_specs=[anywhere] * 5,
        out_specs=(anywhere,) * 4,
        scratch_shapes=[
            pltpu.VMEM((2, K, CX, CY), f32),
            pltpu.VMEM((K, CX, CY), f32),
            pltpu.VMEM((2, K, CX, CY), f32),
            pltpu.SemaphoreType.DMA((3,)),
            pltpu.SemaphoreType.DMA((2, CHUNKS)),
            pltpu.SemaphoreType.DMA((CHUNKS,)),
        ],
        compiler_params=pltpu.CompilerParams(vmem_limit_bytes=VMEM),
    )(*held)


def solution(mesh):
    placed = (
        P(None, None, "gx", "gy"),
        P(None, None, "gx", "gy"),
        P(None, "gx", "gy"),
        P("gx", "gy"),
        P("gx", "gy"),
        P(None, "gx", "gy"),
        P(None, "gx", "gy"),
    )
    return jax.shard_map(
        functools.partial(per_device, mesh.shape["gx"], mesh.shape["gy"]),
        mesh=mesh,
        in_specs=placed,
        out_specs=(
            P("gx", "gy"),
            P(None, "gx", "gy"),
            P(None, "gx", "gy"),
            P(None, None, "gx", "gy"),
        ),
        check_vma=False,
    )
```
